32 devices in a mesh: depth: 2 (over x), row: 4 (over z), col: 4 (over y, core).
Axes of the slice: x: 2, y: 2, z: 4, core: 2. Of those that a mesh axis runs over, the one named last changes fastest.
Arguments:
- context: bfloat16 [1024, 12288], P(('depth', 'row'), 'col'), may hold values from -6 to 6
- d_out: bfloat16 [1024, 12288], P(('depth', 'col'), 'row'), may hold values from -6 to 6
- out_weight: bfloat16 [12288, 12288], P('col', 'row'), may hold values from -0.0546875 to 0.0546875
Outputs:
- d_context: bfloat16 [1024, 12288], P(('depth', 'row'), 'col')
- d_weight: bfloat16 [12288, 12288], P('col', 'row')
The draws below stay inside these ranges and needn't reach their ends.
All inputs are finite; a program needn't handle non-finite values.
Results may differ from the reference program's by a relative error of at most 0.02.
Values may be sent and summed in bfloat16 or wider, within the bound.
A program may use at most 128 MiB of HBM per device.

```python
import jax
import jax.numpy as jnp
from jax import lax

D = 12288
DI = 12288
TOKENS = 1024
N_ROW = 4


def spiked(result, own_key, source, target, blocks, factor):
    def block_of(axis_at):
        return (jnp.arange(result.shape[axis_at]) // (result.shape[axis_at] // blocks)).reshape((-1,) + (1,) * (result.ndim - 1 - axis_at))

    one_side = jax.random.permutation(own_key, blocks)[block_of(target)]
    second = (block_of(target) + blocks // 2) % blocks
    return jnp.where((block_of(source) == one_side) | (block_of(source) == second), factor * result, result)


def block_levels(own_key, extent, split, low, high):
    factor_of, own = 1.0, jax.random.fold_in(own_key, 6)
    for position, parts in split:
        steps = jnp.exp(jax.random.uniform(jax.random.fold_in(own, position), (parts,), jnp.float32, low / len(split), high / len(split)))
        factor_of = factor_of * jnp.repeat(steps, extent[position] // parts).reshape([-1 if axis == position else 1 for axis in range(len(extent))])
    return factor_of


def normal_values(stream_key, shape, width, most, pieces=(), kind=jnp.bfloat16):
    values = jax.random.normal(stream_key, shape, jnp.float32) * width
    if len(pieces) > 0:
        values = block_levels(stream_key, shape, pieces, -0.22, 0.18) * values
    return jnp.clip(values, min=-most, max=most).astype(kind)


def gaussian_with(own_key, extent, width, limit, cuts, heavy, kind=jnp.bfloat16):
    values = width * jax.random.normal(own_key, extent, jnp.float32)
    if cuts:
        values = values * block_levels(own_key, extent, cuts, -0.22, 0.18)
    return jnp.clip(spiked(values, jax.random.fold_in(own_key, 3), *heavy), -limit, limit).astype(kind)


def setup_inputs(seed: int = 0) -> dict:
    seeds = jax.random.split(jax.random.key(seed), 4)
    return {
        "context": normal_values(seeds[0], (TOKENS, DI), 1.0, 6.0, ((0, 8), (1, 4))),
        "d_out": gaussian_with(seeds[1], (TOKENS, D), 1.0, 6.0, ((0, 8), (1, 4)), (1, 0, 8, 2.0)),
        "out_weight": normal_values(seeds[2], (DI, D), D ** -0.5, 0.0546875, ((0, 4), (1, 4))),
    }


def reference(context, d_out, out_weight):
    block = D // N_ROW

    def add_block(total, index):
        start = (index * block).astype(jnp.int32)
        grad_piece = lax.dynamic_slice_in_dim(d_out, start, block, 1)
        weight_piece = lax.dynamic_slice_in_dim(out_weight, start, block, 1)
        partial_value = lax.dot_general(grad_piece, weight_piece, (((1,), (1,)), ((), ())), preferred_element_type=jnp.float32)
        return total + partial_value.astype(jnp.bfloat16).astype(jnp.float32), None

    empty = jnp.zeros((d_out.shape[0], out_weight.shape[0]), jnp.float32)
    d_context, unused = lax.scan(add_block, empty, jnp.arange(N_ROW, dtype=jnp.int32))
    d_weight = lax.dot_general(context, d_out, (((0,), (0,)), ((), ())), preferred_element_type=jnp.float32)
    return d_context.astype(jnp.bfloat16), d_weight.astype(jnp.bfloat16)
```

```python
import jax
import jax.numpy as jnp
from jax import lax
from jax.sharding import PartitionSpec as P


def on_device(context, d_out, out_weight):
    grad_rows = lax.all_gather(d_out, "col", axis=0, tiled=True)
    other_depth = lax.ppermute(d_out, "depth", [(0, 1), (1, 0)])
    other_rows = lax.all_gather(other_depth, "col", axis=0, tiled=True)
    context_rows = lax.all_gather(context, "row", axis=0, tiled=True)
    other_context = lax.ppermute(context_rows, "depth", [(0, 1), (1, 0)])
    d_context = lax.psum_scatter(
        lax.dot_general(
            grad_rows, out_weight, (((1,), (1,)), ((), ())), preferred_element_type=jnp.float32
        ).astype(jnp.bfloat16),
        "row",
        scatter_dimension=0,
        tiled=True,
    )
    d_weight = lax.dot_general(
        jnp.concatenate([context_rows, other_context], axis=0),
        jnp.concatenate([grad_rows, other_rows], axis=0),
        (((0,), (0,)), ((), ())),
        preferred_element_type=jnp.float32,
    ).astype(jnp.bfloat16)
    return (d_context, d_weight)


def solution(mesh):
    in_specs = (P(("depth", "row"), "col"), P(("depth", "col"), "row"), P("col", "row"))
    out_specs = (P(("depth", "row"), "col"), P("col", "row"))
    return jax.shard_map(
        on_device, mesh=mesh, in_specs=in_specs, out_specs=out_specs, check_vma=False
    )
```

```python
import functools

import jax
import jax.numpy as jnp
from jax import lax
from jax.experimental import pallas as pl
from jax.experimental.pallas import tpu as pltpu
from jax.sharding import PartitionSpec as P

MESH = pl.DeviceIdType.MESH
PIECES = 2


def kernel(
    R, C, ctx_in, dout_in, w_in, ctx_all, dout_all, dctx,
    wv, dv, part, sbuf, rbuf,
    w_sem, own_sem, load_sem,
    c_recv, c_right, c_left, c_x,
    g_recv, g_right, g_left, g_core, g_x,
    r_recv, r_send,
):
    T = ctx_in.shape[0]
    tp = T // PIECES
    Y = C // 2
    x, z, c = lax.axis_index("depth"), lax.axis_index("row"), lax.axis_index("col")
    y = c // 2
    core = c - 2 * y
    mate = c + 1 - 2 * core
    halves = range(PIECES)

    to_x, to_core = {"depth": 1 - x}, {"col": mate}
    to_right, to_left = {"row": z + 1}, {"row": z - 1}
    to_yr, to_yl = {"col": c + 2}, {"col": c - 2}

    barrier = pltpu.get_barrier_semaphore()

    def greet(device):
        pl.semaphore_signal(barrier, inc=1, device_id=device, device_id_type=MESH)

    greet(to_x)
    greet(to_core)
    pl.when(z < R - 1)(lambda: greet(to_right))
    pl.when(z > 0)(lambda: greet(to_left))
    pl.when(y < Y - 1)(lambda: greet(to_yr))
    pl.when(y > 0)(lambda: greet(to_yl))
    count = 2
    for there in (z < R - 1, z > 0, y < Y - 1, y > 0):
        count = count + there.astype(jnp.int32)

    wr = w_in.shape[0] // 4
    w_copies = [
        pltpu.make_async_copy(w_in.at[pl.ds(i * wr, wr)], wv.at[pl.ds(i * wr, wr)], w_sem.at[i])
        for i in range(4)
    ]
    own_copies = [
        pltpu.make_async_copy(dout_in, dv.at[pl.ds(c * T, T)], own_sem.at[0]),
        pltpu.make_async_copy(dout_in, dout_all.at[pl.ds((x * C + c) * T, T)], own_sem.at[1]),
        pltpu.make_async_copy(ctx_in, ctx_all.at[pl.ds((x * R + z) * T, T)], own_sem.at[2]),
    ]
    for copy in [own_copies[0]] + w_copies + own_copies[1:]:
        copy.start()

    def rows(block, p):
        return pl.ds(block * T + p * tp, tp)

    def depth_of(k):
        return x if k == 0 else 1 - x

    def remote(src, dst, send, recv, device):
        return pltpu.make_async_remote_copy(
            src_ref=src, dst_ref=dst, send_sem=send, recv_sem=recv, device_id=device, device_id_type=MESH
        )

    def c_copy(way, r, p, own=False):
        dst = ctx_all.at[rows(x * R + r, p)]
        src = ctx_in.at[rows(0, p)] if own else dst
        if way == "x":
            return remote(src, dst, c_x.at[r, p], c_recv.at[1, r, p], to_x)
        if way == "right":
            return remote(src, dst, c_right.at[r, p], c_recv.at[0, r, p], to_right)
        return remote(src, dst, c_left.at[r, p], c_recv.at[0, r, p], to_left)

    def c_wait(k, r, p):
        there = ctx_all.at[rows(depth_of(k) * R + r, p)]
        remote(there, there, c_x.at[r, p], c_recv.at[k, r, p], to_x).wait_recv()

    def g_copy(way, k, b, p, own=False):
        dst = dout_all.at[rows(depth_of(k) * C + b, p)]
        src = dout_in.at[rows(0, p)] if own else dst
        if way == "x":
            return remote(src, dst, g_x.at[p], g_recv.at[1, b, p], to_x)
        send, device = {"right": (g_right, to_yr), "left": (g_left, to_yl), "core": (g_core, to_core)}[way]
        return remote(src, dst, send.at[k, b, p], g_recv.at[k, b, p], device)

    def g_wait(k, b, p):
        there = dout_all.at[rows(depth_of(k) * C + b, p)]
        remote(there, there, g_core.at[k, b, p], g_recv.at[k, b, p], to_core).wait_recv()

    def g_sends(k, b, p, own=False):
        pl.when(y < Y - 1)(lambda: g_copy("right", k, b, p, own).start())
        pl.when(y > 0)(lambda: g_copy("left", k, b, p, own).start())
        g_copy("core", k, b, p, own).start()

    pl.semaphore_wait(barrier, count)

    for p in halves:
        g_sends(0, c, p, own=True)
        g_copy("x", 0, c, p, own=True).start()
    for p in halves:
        pl.when(z < R - 1)(lambda: c_copy("right", z, p, own=True).start())
        pl.when(z > 0)(lambda: c_copy("left", z, p, own=True).start())
        c_copy("x", z, p, own=True).start()

    def c_step(s):
        def arrived(r, way, more):
            for p in halves:
                c_wait(0, r, p)
                pl.when(more)(lambda: c_copy(way, r, p).start())
                c_copy("x", r, p).start()

        pl.when(z - 1 - s >= 0)(lambda: arrived(z - 1 - s, "right", z < R - 1))
        pl.when(z + 1 + s <= R - 1)(lambda: arrived(z + 1 + s, "left", z > 0))

    def g_step(k, s):
        def arrived(b, way, more):
            for p in halves:
                g_wait(k, b, p)
                pl.when(more)(lambda: g_copy(way, k, b, p).start())
                g_copy("core", k, b, p).start()

        pl.when(y - 1 - s >= 0)(lambda: arrived(c - 2 - 2 * s, "right", y < Y - 1))
        pl.when(y + 1 + s <= Y - 1)(lambda: arrived(c + 2 + 2 * s, "left", y > 0))

    def load(block, count_of, which):
        return pltpu.make_async_copy(
            dout_all.at[pl.ds((x * C + block) * T, count_of * T)],
            dv.at[pl.ds(block * T, count_of * T)],
            load_sem.at[which],
        )

    tn = 512 if wv.shape[0] % 512 == 0 else 256

    def multiply(pair):
        tokens = pl.ds(pair * 2 * T, 2 * T)

        @pl.loop(0, wv.shape[0] // tn)
        def _(i):
            columns = pl.ds(pl.multiple_of(i * tn, tn), tn)
            part[tokens, columns] = lax.dot_general(
                dv[tokens, :], wv[columns, :], (((1,), (1,)), ((), ())), preferred_element_type=jnp.float32
            )

    for p in halves:
        g_wait(0, mate, p)
    load(mate, 1, 0).start()
    own_copies[0].wait()
    for copy in w_copies:
        copy.wait()
    load(mate, 1, 0).wait()
    multiply(y)

    c_step(0)
    for p in halves:
        g_wait(1, c, p)
        g_sends(1, c, p)

    def far_pair(s):
        def take(pair, which):
            for p in halves:
                g_wait(0, 2 * pair + 1 - core, p)
            load(2 * pair, 2, which).start()
            load(2 * pair, 2, which).wait()
            multiply(pair)

        pl.when(y - 1 - s >= 0)(lambda: take(y - 1 - s, 1))
        pl.when(y + 1 + s <= Y - 1)(lambda: take(y + 1 + s, 2))

    for s in range(Y - 1):
        g_step(0, s)
        far_pair(s)

    def r_copy(d, p, rightward):
        if rightward:
            return remote(sbuf.at[rows(d, p)], rbuf.at[rows(d, p)], r_send.at[d, p], r_recv.at[d, p], to_right)
        slot = jnp.where(z - 1 == d, R, d)
        return remote(sbuf.at[rows(d, p)], rbuf.at[rows(slot, p)], r_send.at[d, p], r_recv.at[slot, p], to_left)

    def r_wait(slot, p):
        there = rbuf.at[rows(slot, p)]
        remote(there, there, r_send.at[0, p], r_recv.at[slot, p], to_x).wait_recv()

    def r_hop(d, p, rightward, first):
        if first:
            sbuf[rows(d, p), :] = part[rows(d, p), :].astype(jnp.bfloat16)
        else:
            r_wait(d, p)
            total = part[rows(d, p), :] + rbuf[rows(d, p), :].astype(jnp.float32)
            sbuf[rows(d, p), :] = total.astype(jnp.bfloat16)
        r_copy(d, p, rightward).start()

    @pl.when(z == 0)
    def _():
        for d in range(R - 1, 0, -1):
            for p in halves:
                r_hop(d, p, True, True)

    @pl.when(z == R - 1)
    def _():
        for d in range(R - 1):
            for p in halves:
                r_hop(d, p, False, True)

    for s in range(1, R - 1):
        c_step(s)
    for s in range(Y - 1):
        g_step(1, s)

    for i in range(R - 1):
        for p in halves:
            pl.when((z > 0) & (z < R - 1 - i))(lambda: r_hop(R - 1 - i, p, True, False))
            pl.when((z < R - 1) & (z > i))(lambda: r_hop(i, p, False, False))

    def own_rows(slot, p):
        return pl.ds(pl.multiple_of(slot * T + p * tp, tp), tp)

    for p in halves:
        out = pl.ds(p * tp, tp)

        @pl.when(z == 0)
        def _():
            r_wait(R, p)
            dctx[out, :] = (part[own_rows(z, p), :] + rbuf[own_rows(R, p), :].astype(jnp.float32)).astype(jnp.bfloat16)

        @pl.when(z == R - 1)
        def _():
            r_wait(z, p)
            dctx[out, :] = (part[own_rows(z, p), :] + rbuf[own_rows(z, p), :].astype(jnp.float32)).astype(jnp.bfloat16)

        @pl.when((z > 0) & (z < R - 1))
        def _():
            r_wait(z, p)
            r_wait(R, p)
            both = rbuf[own_rows(z, p), :].astype(jnp.float32) + rbuf[own_rows(R, p), :].astype(jnp.float32)
            dctx[out, :] = (part[own_rows(z, p), :] + both).astype(jnp.bfloat16)

    for p in halves:
        for b in range(Y):
            g_wait(1, 2 * b + 1 - core, p)
        for r in range(R):
            c_wait(1, r, p)
    own_copies[1].wait()
    own_copies[2].wait()
    for p in halves:
        g_copy("x", 0, c, p).wait_send()
        for k in range(2):
            for b in range(Y):
                block = 2 * b + core
                g_copy("core", k, block, p).wait_send()
                pl.when((y < Y - 1) & (b <= y))(lambda: g_copy("right", k, block, p).wait_send())
                pl.when((y > 0) & (b >= y))(lambda: g_copy("left", k, block, p).wait_send())
        for r in range(R):
            c_copy("x", r, p).wait_send()
            pl.when((z < R - 1) & (r <= z))(lambda: c_copy("right", r, p).wait_send())
            pl.when((z > 0) & (r >= z))(lambda: c_copy("left", r, p).wait_send())
            pl.when(z != r)(lambda: r_copy(r, p, True).wait_send())


def exchange(R, C, context, d_out, out_weight):
    T, FC = context.shape
    FR = d_out.shape[1]
    bf16, dma = jnp.bfloat16, pltpu.SemaphoreType.DMA
    hbm, vmem = pl.BlockSpec(memory_space=pl.ANY), pl.BlockSpec(memory_space=pltpu.VMEM)
    return pl.pallas_call(
        functools.partial(kernel, R, C),
        out_shape=(
            jax.ShapeDtypeStruct((2 * R * T, FC), bf16),
            jax.ShapeDtypeStruct((2 * C * T, FR), bf16),
            jax.ShapeDtypeStruct((T, FC), bf16),
        ),
        in_specs=[hbm, hbm, hbm],
        out_specs=(hbm, hbm, vmem),
        scratch_shapes=[
            pltpu.VMEM((FC, FR), bf16),
            pltpu.VMEM((C * T, FR), bf16),
            pltpu.VMEM((C * T, FC), jnp.float32),
            pltpu.VMEM((R * T, FC), bf16),
            pltpu.VMEM(((R + 1) * T, FC), bf16),
            dma((4,)), dma((3,)), dma((3,)),
            dma((2, R, PIECES)), dma((R, PIECES)), dma((R, PIECES)), dma((R, PIECES)),
            dma((2, C, PIECES)), dma((2, C, PIECES)), dma((2, C, PIECES)), dma((2, C, PIECES)), dma((PIECES,)),
            dma((R + 1, PIECES)), dma((R, PIECES)),
        ],
        compiler_params=pltpu.CompilerParams(
            collective_id=0, has_side_effects=True, vmem_limit_bytes=56 * 1024 * 1024
        ),
        cost_estimate=pl.CostEstimate(
            flops=2 * C * T * FC * FR, bytes_accessed=2 * FC * FR, transcendentals=0
        ),
    )(context, d_out, out_weight)


def on_device(R, C, context, d_out, out_weight):
    context_rows, grad_rows, d_context = exchange(R, C, context, d_out, out_weight)
    d_weight = lax.dot_general(
        context_rows, grad_rows, (((0,), (0,)), ((), ())), preferred_element_type=jnp.float32
    ).astype(jnp.bfloat16)
    return (d_context, d_weight)


def solution(mesh):
    in_specs = (P(("depth", "row"), "col"), P(("depth", "col"), "row"), P("col", "row"))
    out_specs = (P(("depth", "row"), "col"), P("col", "row"))
    return jax.shard_map(
        functools.partial(on_device, mesh.shape["row"], mesh.shape["col"]),
        mesh=mesh, in_specs=in_specs, out_specs=out_specs, check_vma=False,
    )
```

```python
import functools

import jax
import jax.numpy as jnp
from jax import lax
from jax.experimental import pallas as pl
from jax.experimental.pallas import tpu as pltpu
from jax.sharding import PartitionSpec as P

MESH = pl.DeviceIdType.MESH
PIECES = 2


def kernel(
    R, C, ctx_in, dout_in, w_in, ctx_other, dout_other, dctx, half_weight,
    wv, cv, dv, part, sbuf, rbuf, turned, stage,
    w_sem, own_sem, stage_sem,
    c_recv, c_right, c_left, c_x,
    g_recv, g_right, g_left, g_core, g_x,
    r_recv, r_send,
):
    T = ctx_in.shape[0]
    tp = T // PIECES
    Y = C // 2
    x, z, c = lax.axis_index("depth"), lax.axis_index("row"), lax.axis_index("col")
    y = c // 2
    core = c - 2 * y
    mate = c + 1 - 2 * core
    halves = range(PIECES)
    cuts = [(0, T // 8), (T // 8, T // 2 - T // 8), (T // 2, T // 2)]
    late = range(1, 3)

    to_x, to_core = {"depth": 1 - x}, {"col": mate}
    to_right, to_left = {"row": z + 1}, {"row": z - 1}
    to_yr, to_yl = {"col": c + 2}, {"col": c - 2}

    barrier = pltpu.get_barrier_semaphore()

    def greet(device):
        pl.semaphore_signal(barrier, inc=1, device_id=device, device_id_type=MESH)

    greet(to_x)
    greet(to_core)
    pl.when(z < R - 1)(lambda: greet(to_right))
    pl.when(z > 0)(lambda: greet(to_left))
    pl.when(y < Y - 1)(lambda: greet(to_yr))
    pl.when(y > 0)(lambda: greet(to_yl))
    count = 2
    for there in (z < R - 1, z > 0, y < Y - 1, y > 0):
        count = count + there.astype(jnp.int32)

    wr = w_in.shape[0] // 4
    w_copies = [
        pltpu.make_async_copy(w_in.at[pl.ds(i * wr, wr)], wv.at[pl.ds(i * wr, wr)], w_sem.at[i])
        for i in range(4)
    ]
    own_copies = [
        pltpu.make_async_copy(dout_in, dv.at[pl.ds(c * T, T)], own_sem.at[0]),
        pltpu.make_async_copy(ctx_in, cv.at[pl.ds(z * T, T)], own_sem.at[1]),
    ]
    for copy in [own_copies[0]] + w_copies + own_copies[1:]:
        copy.start()

    def rows(block, p):
        return pl.ds(block * T + p * tp, tp)

    def remote(src, dst, send, recv, device):
        return pltpu.make_async_remote_copy(
            src_ref=src, dst_ref=dst, send_sem=send, recv_sem=recv, device_id=device, device_id_type=MESH
        )

    def c_rows(r, p):
        return pl.ds(r * T + cuts[p][0], cuts[p][1])

    def c_copy(way, k, r, p, own=False):
        there = (cv, ctx_other)[k].at[c_rows(r, p)]
        src = ctx_in.at[c_rows(0, p)] if own else there
        if way == "x":
            return remote(src, ctx_other.at[c_rows(r, p)], c_x.at[r, p], c_recv.at[1, r, p], to_x)
        send, device = (c_right, to_right) if way == "right" else (c_left, to_left)
        return remote(src, there, send.at[k, r, p], c_recv.at[k, r, p], device)

    def c_wait(k, r, p):
        there = (cv, ctx_other)[k].at[c_rows(r, p)]
        remote(there, there, c_x.at[r, p], c_recv.at[k, r, p], to_x).wait_recv()

    def g_copy(way, k, b, p, own=False):
        there = (dv, dout_other)[k].at[rows(b, p)]
        src = dout_in.at[rows(0, p)] if own else there
        if way == "x":
            return remote(src, dout_other.at[rows(b, p)], g_x.at[p], g_recv.at[1, b, p], to_x)
        send, device = {"right": (g_right, to_yr), "left": (g_left, to_yl), "core": (g_core, to_core)}[way]
        return remote(src, there, send.at[k, b, p], g_recv.at[k, b, p], device)

    def g_wait(k, b, p):
        there = (dv, dout_other)[k].at[rows(b, p)]
        remote(there, there, g_core.at[k, b, p], g_recv.at[k, b, p], to_core).wait_recv()

    def g_sends(k, b, p, own=False):
        pl.when(y < Y - 1)(lambda: g_copy("right", k, b, p, own).start())
        pl.when(y > 0)(lambda: g_copy("left", k, b, p, own).start())
        g_copy("core", k, b, p, own).start()

    pl.semaphore_wait(barrier, count)

    for p in halves:
        g_sends(0, c, p, own=True)
        g_copy("x", 0, c, p, own=True).start()

    def c_sends(k, p, own):
        pl.when(z < R - 1)(lambda: c_copy("right", k, z, p, own).start())
        pl.when(z > 0)(lambda: c_copy("left", k, z, p, own).start())

    for p in range(3):
        c_copy("x", 0, z, p, own=True).start()
        c_sends(0, p, own=True)

    def c_step(s):
        def arrived(r, way, more):
            for k, p in ((0, 0), (0, 1), (0, 2), (1, 0)):
                c_wait(k, r, p)
                pl.when(more)(lambda: c_copy(way, k, r, p).start())
                if p > 0:
                    c_copy("x", 0, r, p).start()

        pl.when(z - 1 - s >= 0)(lambda: arrived(z - 1 - s, "right", z < R - 1))
        pl.when(z + 1 + s <= R - 1)(lambda: arrived(z + 1 + s, "left", z > 0))

    def g_step(k, s):
        def arrived(b, way, more):
            for p in halves:
                g_wait(k, b, p)
                pl.when(more)(lambda: g_copy(way, k, b, p).start())
                g_copy("core", k, b, p).start()

        pl.when(y - 1 - s >= 0)(lambda: arrived(c - 2 - 2 * s, "right", y < Y - 1))
        pl.when(y + 1 + s <= Y - 1)(lambda: arrived(c + 2 + 2 * s, "left", y > 0))

    tn = 512 if wv.shape[0] % 512 == 0 else 256

    def multiply(pair):
        tokens = pl.ds(pair * 2 * T, 2 * T)

        @pl.loop(0, wv.shape[0] // tn)
        def _(i):
            columns = pl.ds(pl.multiple_of(i * tn, tn), tn)
            part[tokens, columns] = lax.dot_general(
                dv[tokens, :], wv[columns, :], (((1,), (1,)), ((), ())), preferred_element_type=jnp.float32
            )

    for p in halves:
        g_wait(0, mate, p)
    own_copies[0].wait()
    for copy in w_copies:
        copy.wait()
    multiply(y)

    for p in halves:
        g_wait(1, c, p)
        g_sends(1, c, p)
    c_wait(1, z, 0)
    c_sends(1, 0, own=False)
    c_step(0)

    def far_pair(s):
        def take(pair):
            for p in halves:
                g_wait(0, 2 * pair + 1 - core, p)
            multiply(pair)

        pl.when(y - 1 - s >= 0)(lambda: take(y - 1 - s))
        pl.when(y + 1 + s <= Y - 1)(lambda: take(y + 1 + s))

    for s in range(Y - 1):
        g_step(0, s)
        far_pair(s)

    def r_copy(d, p, rightward):
        if rightward:
            return remote(sbuf.at[rows(d, p)], rbuf.at[rows(d, p)], r_send.at[d, p], r_recv.at[d, p], to_right)
        slot = jnp.where(z - 1 == d, R, d)
        return remote(sbuf.at[rows(d, p)], rbuf.at[rows(slot, p)], r_send.at[d, p], r_recv.at[slot, p], to_left)

    def r_wait(slot, p):
        there = rbuf.at[rows(slot, p)]
        remote(there, there, r_send.at[0, p], r_recv.at[slot, p], to_x).wait_recv()

    def r_hop(d, p, rightward, first):
        if first:
            sbuf[rows(d, p), :] = part[rows(d, p), :].astype(jnp.bfloat16)
        else:
            r_wait(d, p)
            total = part[rows(d, p), :] + rbuf[rows(d, p), :].astype(jnp.float32)
            sbuf[rows(d, p), :] = total.astype(jnp.bfloat16)
        r_copy(d, p, rightward).start()

    @pl.when(z == 0)
    def _():
        for d in range(R - 1, 0, -1):
            for p in halves:
                r_hop(d, p, True, True)

    @pl.when(z == R - 1)
    def _():
        for d in range(R - 1):
            for p in halves:
                r_hop(d, p, False, True)

    for s in range(1, R - 1):
        c_step(s)
    for s in range(Y - 1):
        g_step(1, s)

    own_copies[1].wait()
    stripes = cv.shape[1] // tn

    def stage_copy(i):
        return pltpu.make_async_copy(
            stage.at[i % 2], half_weight.at[pl.ds(i * tn, tn)], stage_sem.at[i % 2]
        )

    def stripe(i):
        if i >= 2:
            stage_copy(i - 2).wait()
        turned[...] = cv[:, pl.ds(i * tn, tn)].T

        @pl.loop(0, dv.shape[1] // tn)
        def _(j):
            columns = pl.ds(pl.multiple_of(j * tn, tn), tn)
            stage[i % 2, :, columns] = jnp.dot(
                turned[...], dv[:, columns], preferred_element_type=jnp.float32
            ).astype(jnp.bfloat16)

        stage_copy(i).start()

    for i in range(R - 1):
        if i < stripes // 2:
            stripe(i)
        for p in halves:
            pl.when((z > 0) & (z < R - 1 - i))(lambda: r_hop(R - 1 - i, p, True, False))
            pl.when((z < R - 1) & (z > i))(lambda: r_hop(i, p, False, False))

    def own_rows(slot, p):
        return pl.ds(pl.multiple_of(slot * T + p * tp, tp), tp)

    for p in halves:
        out = pl.ds(p * tp, tp)

        @pl.when(z == 0)
        def _():
            r_wait(R, p)
            dctx[out, :] = (part[own_rows(z, p), :] + rbuf[own_rows(R, p), :].astype(jnp.float32)).astype(jnp.bfloat16)

        @pl.when(z == R - 1)
        def _():
            r_wait(z, p)
            dctx[out, :] = (part[own_rows(z, p), :] + rbuf[own_rows(z, p), :].astype(jnp.float32)).astype(jnp.bfloat16)

        @pl.when((z > 0) & (z < R - 1))
        def _():
            r_wait(z, p)
            r_wait(R, p)
            both = rbuf[own_rows(z, p), :].astype(jnp.float32) + rbuf[own_rows(R, p), :].astype(jnp.float32)
            dctx[out, :] = (part[own_rows(z, p), :] + both).astype(jnp.bfloat16)

    for i in range(min(R - 1, stripes // 2), stripes):
        stripe(i)
    for i in range(max(stripes - 2, 0), stripes):
        stage_copy(i).wait()

    for p in halves:
        for b in range(Y):
            g_wait(1, 2 * b + 1 - core, p)
    for p in late:
        for r in range(R):
            c_wait(1, r, p)
    for p in halves:
        g_copy("x", 0, c, p).wait_send()
        for k in range(2):
            for b in range(Y):
                block = 2 * b + core
                g_copy("core", k, block, p).wait_send()
                pl.when((y < Y - 1) & (b <= y))(lambda: g_copy("right", k, block, p).wait_send())
                pl.when((y > 0) & (b >= y))(lambda: g_copy("left", k, block, p).wait_send())
        for r in range(R):
            pl.when(z != r)(lambda: r_copy(r, p, True).wait_send())
    c_copy("x", 0, z, 0).wait_send()
    for p in late:
        for r in range(R):
            c_copy("x", 0, r, p).wait_send()
    for k, p in ((0, 0), (0, 1), (0, 2), (1, 0)):
        for r in range(R):
            pl.when((z < R - 1) & (r <= z))(lambda: c_copy("right", k, r, p).wait_send())
            pl.when((z > 0) & (r >= z))(lambda: c_copy("left", k, r, p).wait_send())


def exchange(R, C, context, d_out, out_weight):
    T, FC = context.shape
    FR = d_out.shape[1]
    tn = 512 if FC % 512 == 0 else 256
    bf16, dma = jnp.bfloat16, pltpu.SemaphoreType.DMA
    hbm, vmem = pl.BlockSpec(memory_space=pl.ANY), pl.BlockSpec(memory_space=pltpu.VMEM)
    return pl.pallas_call(
        functools.partial(kernel, R, C),
        out_shape=(
            jax.ShapeDtypeStruct((R * T, FC), bf16),
            jax.ShapeDtypeStruct((C * T, FR), bf16),
            jax.ShapeDtypeStruct((T, FC), bf16),
            jax.ShapeDtypeStruct((FC, FR), bf16),
        ),
        in_specs=[hbm, hbm, hbm],
        out_specs=(hbm, hbm, vmem, hbm),
        scratch_shapes=[
            pltpu.VMEM((FC, FR), bf16),
            pltpu.VMEM((R * T, FC), bf16),
            pltpu.VMEM((C * T, FR), bf16),
            pltpu.VMEM((C * T, FC), jnp.float32),
            pltpu.VMEM((R * T, FC), bf16),
            pltpu.VMEM(((R + 1) * T, FC), bf16),
            pltpu.VMEM((tn, R * T), bf16),
            pltpu.VMEM((2, tn, FR), bf16),
            dma((4,)), dma((2,)), dma((2,)),
            dma((2, R, 3)), dma((2, R, 3)), dma((2, R, 3)), dma((R, 3)),
            dma((2, C, PIECES)), dma((2, C, PIECES)), dma((2, C, PIECES)), dma((2, C, PIECES)), dma((PIECES,)),
            dma((R + 1, PIECES)), dma((R, PIECES)),
        ],
        compiler_params=pltpu.CompilerParams(
            collective_id=0, has_side_effects=True, vmem_limit_bytes=56 * 1024 * 1024
        ),
        cost_estimate=pl.CostEstimate(
            flops=4 * C * T * FC * FR, bytes_accessed=4 * FC * FR, transcendentals=0
        ),
    )(context, d_out, out_weight)


def on_device(R, C, context, d_out, out_weight):
    context_rows, grad_rows, d_context, half_weight = exchange(R, C, context, d_out, out_weight)
    other_half = lax.dot_general(
        context_rows, grad_rows, (((0,), (0,)), ((), ())), preferred_element_type=jnp.float32
    )
    d_weight = (half_weight.astype(jnp.float32) + other_half).astype(jnp.bfloat16)
    return (d_context, d_weight)


def solution(mesh):
    in_specs = (P(("depth", "row"), "col"), P(("depth", "col"), "row"), P("col", "row"))
    out_specs = (P(("depth", "row"), "col"), P("col", "row"))
    return jax.shard_map(
        functools.partial(on_device, mesh.shape["row"], mesh.shape["col"]),
        mesh=mesh, in_specs=in_specs, out_specs=out_specs, check_vma=False,
    )
```

```python
import functools

import jax
import jax.numpy as jnp
from jax import lax
from jax.experimental import pallas as pl
from jax.experimental.pallas import tpu as pltpu
from jax.sharding import PartitionSpec as P

MESH = pl.DeviceIdType.MESH
PIECES = 2


def kernel(
    R, C, ctx_in, dout_in, w_in, ctx_other, dout_other, dctx, half_weight,
    wv, cv, dv, part, sbuf, rbuf, turned, stage,
    w_sem, own_sem, stage_sem,
    c_recv, c_right, c_left, c_x,
    g_recv, g_right, g_left, g_core, g_x,
    r_recv, r_send,
):
    T = ctx_in.shape[0]
    tp = T // PIECES
    Y = C // 2
    x, z, c = lax.axis_index("depth"), lax.axis_index("row"), lax.axis_index("col")
    y = c // 2
    core = c - 2 * y
    mate = c + 1 - 2 * core
    halves = range(PIECES)

    to_x, to_core = {"depth": 1 - x}, {"col": mate}
    to_right, to_left = {"row": z + 1}, {"row": z - 1}
    to_yr, to_yl = {"col": c + 2}, {"col": c - 2}

    barrier = pltpu.get_barrier_semaphore()

    def greet(device):
        pl.semaphore_signal(barrier, inc=1, device_id=device, device_id_type=MESH)

    greet(to_x)
    greet(to_core)
    pl.when(z < R - 1)(lambda: greet(to_right))
    pl.when(z > 0)(lambda: greet(to_left))
    pl.when(y < Y - 1)(lambda: greet(to_yr))
    pl.when(y > 0)(lambda: greet(to_yl))
    count = 2
    for there in (z < R - 1, z > 0, y < Y - 1, y > 0):
        count = count + there.astype(jnp.int32)

    wr = w_in.shape[0] // 4
    w_copies = [
        pltpu.make_async_copy(w_in.at[pl.ds(i * wr, wr)], wv.at[pl.ds(i * wr, wr)], w_sem.at[i])
        for i in range(4)
    ]
    own_copies = [
        pltpu.make_async_copy(dout_in, dv.at[pl.ds(c * T, T)], own_sem.at[0]),
        pltpu.make_async_copy(ctx_in, cv.at[pl.ds(z * T, T)], own_sem.at[1]),
    ]
    for copy in [own_copies[0]] + w_copies + own_copies[1:]:
        copy.start()

    def rows(block, p):
        return pl.ds(block * T + p * tp, tp)

    def remote(src, dst, send, recv, device):
        return pltpu.make_async_remote_copy(
            src_ref=src, dst_ref=dst, send_sem=send, recv_sem=recv, device_id=device, device_id_type=MESH
        )

    def c_rows(r, p):
        return rows(r, p)

    def c_copy(way, k, r, p, own=False):
        there = (cv, ctx_other)[k].at[c_rows(r, p)]
        src = ctx_in.at[c_rows(0, p)] if own else there
        if way == "x":
            return remote(src, ctx_other.at[c_rows(r, p)], c_x.at[r, p], c_recv.at[1, r, p], to_x)
        send, device = (c_right, to_right) if way == "right" else (c_left, to_left)
        return remote(src, there, send.at[k, r, p], c_recv.at[k, r, p], device)

    def c_wait(k, r, p):
        there = (cv, ctx_other)[k].at[c_rows(r, p)]
        remote(there, there, c_x.at[r, p], c_recv.at[k, r, p], to_x).wait_recv()

    def g_copy(way, k, b, p, own=False):
        there = (dv, dout_other)[k].at[rows(b, p)]
        src = dout_in.at[rows(0, p)] if own else there
        if way == "x":
            return remote(src, dout_other.at[rows(b, p)], g_x.at[p], g_recv.at[1, b, p], to_x)
        send, device = {"right": (g_right, to_yr), "left": (g_left, to_yl), "core": (g_core, to_core)}[way]
        return remote(src, there, send.at[k, b, p], g_recv.at[k, b, p], device)

    def g_wait(k, b, p):
        there = (dv, dout_other)[k].at[rows(b, p)]
        remote(there, there, g_core.at[k, b, p], g_recv.at[k, b, p], to_core).wait_recv()

    def g_sends(k, b, p, own=False):
        pl.when(y < Y - 1)(lambda: g_copy("right", k, b, p, own).start())
        pl.when(y > 0)(lambda: g_copy("left", k, b, p, own).start())
        g_copy("core", k, b, p, own).start()

    pl.semaphore_wait(barrier, count)

    for p in halves:
        g_sends(0, c, p, own=True)
        g_copy("x", 0, c, p, own=True).start()

    def c_sends(k, p, own):
        pl.when(z < R - 1)(lambda: c_copy("right", k, z, p, own).start())
        pl.when(z > 0)(lambda: c_copy("left", k, z, p, own).start())

    for p in halves:
        c_copy("x", 0, z, p, own=True).start()
        c_sends(0, p, own=True)

    def c_step(s):
        def arrived(r, way, more):
            for p in halves:
                c_wait(0, r, p)
                pl.when(more)(lambda: c_copy(way, 0, r, p).start())
                c_copy("x", 0, r, p).start()

        pl.when(z - 1 - s >= 0)(lambda: arrived(z - 1 - s, "right", z < R - 1))
        pl.when(z + 1 + s <= R - 1)(lambda: arrived(z + 1 + s, "left", z > 0))

    def g_step(k, s):
        def arrived(b, way, more):
            for p in halves:
                g_wait(k, b, p)
                pl.when(more)(lambda: g_copy(way, k, b, p).start())
                g_copy("core", k, b, p).start()

        pl.when(y - 1 - s >= 0)(lambda: arrived(c - 2 - 2 * s, "right", y < Y - 1))
        pl.when(y + 1 + s <= Y - 1)(lambda: arrived(c + 2 + 2 * s, "left", y > 0))

    tn = 512 if wv.shape[0] % 512 == 0 else 256

    def multiply(pair):
        tokens = pl.ds(pair * 2 * T, 2 * T)

        @pl.loop(0, wv.shape[0] // tn)
        def _(i):
            columns = pl.ds(pl.multiple_of(i * tn, tn), tn)
            part[tokens, columns] = lax.dot_general(
                dv[tokens, :], wv[columns, :], (((1,), (1,)), ((), ())), preferred_element_type=jnp.float32
            )

    def own_rows(slot, p):
        return pl.ds(pl.multiple_of(slot * T + p * tp, tp), tp)

    def r_copy(d, p, rightward):
        if rightward:
            return remote(sbuf.at[rows(d, p)], rbuf.at[rows(d, p)], r_send.at[d, p], r_recv.at[d, p], to_right)
        slot = jnp.where(z - 1 == d, R, d)
        return remote(sbuf.at[rows(d, p)], rbuf.at[rows(slot, p)], r_send.at[d, p], r_recv.at[slot, p], to_left)

    def r_wait(slot, p):
        there = rbuf.at[rows(slot, p)]
        remote(there, there, r_send.at[0, p], r_recv.at[slot, p], to_x).wait_recv()

    def r_hop(d, p, rightward, first):
        here = own_rows(d, p)
        if first:
            sbuf[here, :] = part[here, :].astype(jnp.bfloat16)
        else:
            r_wait(d, p)
            sbuf[here, :] = (part[here, :] + rbuf[here, :].astype(jnp.float32)).astype(jnp.bfloat16)
        r_copy(d, p, rightward).start()

    def r_begin(pair):
        def both(d, rightward):
            for p in halves:
                r_hop(d, p, rightward, True)

        for d in (2 * pair + 1, 2 * pair):
            pl.when((z == 0) & (d > 0))(lambda: both(d, True))
        for d in (2 * pair, 2 * pair + 1):
            pl.when((z == R - 1) & (d < R - 1))(lambda: both(d, False))

    for p in halves:
        g_wait(0, mate, p)
    own_copies[0].wait()
    for copy in w_copies:
        copy.wait()
    multiply(y)
    r_begin(y)

    for p in halves:
        g_wait(1, c, p)
        g_sends(1, c, p)
    c_step(0)

    def far_pair(s):
        def take(pair):
            for p in halves:
                g_wait(0, 2 * pair + 1 - core, p)
            multiply(pair)
            r_begin(pair)

        pl.when(y - 1 - s >= 0)(lambda: take(y - 1 - s))
        pl.when(y + 1 + s <= Y - 1)(lambda: take(y + 1 + s))

    for s in range(Y - 1):
        g_step(0, s)
        far_pair(s)

    for s in range(1, R - 1):
        c_step(s)
    for s in range(Y - 1):
        g_step(1, s)

    own_copies[1].wait()
    stripes = cv.shape[1] // tn

    def stage_copy(i):
        return pltpu.make_async_copy(
            stage.at[i % 2], half_weight.at[pl.ds(i * tn, tn)], stage_sem.at[i % 2]
        )

    def stripe(i):
        if i >= 2:
            stage_copy(i - 2).wait()
        turned[...] = cv[:, pl.ds(i * tn, tn)].T

        @pl.loop(0, dv.shape[1] // tn)
        def _(j):
            columns = pl.ds(pl.multiple_of(j * tn, tn), tn)
            stage[i % 2, :, columns] = jnp.dot(
                turned[...], dv[:, columns], preferred_element_type=jnp.float32
            ).astype(jnp.bfloat16)

        stage_copy(i).start()

    for i in range(R - 1):
        if i == 1:
            stripe(0)
        for p in halves:
            pl.when((z > 0) & (z < R - 1 - i))(lambda: r_hop(R - 1 - i, p, True, False))
            pl.when((z < R - 1) & (z > i))(lambda: r_hop(i, p, False, False))

    for i in range(1, stripes):
        stripe(i)

    for p in halves:
        out = pl.ds(p * tp, tp)

        @pl.when(z == 0)
        def _():
            r_wait(R, p)
            dctx[out, :] = (part[own_rows(z, p), :] + rbuf[own_rows(R, p), :].astype(jnp.float32)).astype(jnp.bfloat16)

        @pl.when(z == R - 1)
        def _():
            r_wait(z, p)
            dctx[out, :] = (part[own_rows(z, p), :] + rbuf[own_rows(z, p), :].astype(jnp.float32)).astype(jnp.bfloat16)

        @pl.when((z > 0) & (z < R - 1))
        def _():
            r_wait(z, p)
            r_wait(R, p)
            both = rbuf[own_rows(z, p), :].astype(jnp.float32) + rbuf[own_rows(R, p), :].astype(jnp.float32)
            dctx[out, :] = (part[own_rows(z, p), :] + both).astype(jnp.bfloat16)

    for i in range(max(stripes - 2, 0), stripes):
        stage_copy(i).wait()

    for p in halves:
        for b in range(Y):
            g_wait(1, 2 * b + 1 - core, p)
    for p in halves:
        for r in range(R):
            c_wait(1, r, p)
    for p in halves:
        g_copy("x", 0, c, p).wait_send()
        for k in range(2):
            for b in range(Y):
                block = 2 * b + core
                g_copy("core", k, block, p).wait_send()
                pl.when((y < Y - 1) & (b <= y))(lambda: g_copy("right", k, block, p).wait_send())
                pl.when((y > 0) & (b >= y))(lambda: g_copy("left", k, block, p).wait_send())
        for r in range(R):
            pl.when(z != r)(lambda: r_copy(r, p, True).wait_send())
    for p in halves:
        for r in range(R):
            c_copy("x", 0, r, p).wait_send()
    for p in halves:
        for r in range(R):
            pl.when((z < R - 1) & (r <= z))(lambda: c_copy("right", 0, r, p).wait_send())
            pl.when((z > 0) & (r >= z))(lambda: c_copy("left", 0, r, p).wait_send())


def exchange(R, C, context, d_out, out_weight):
    T, FC = context.shape
    FR = d_out.shape[1]
    tn = 512 if FC % 512 == 0 else 256
    bf16, dma = jnp.bfloat16, pltpu.SemaphoreType.DMA
    hbm, vmem = pl.BlockSpec(memory_space=pl.ANY), pl.BlockSpec(memory_space=pltpu.VMEM)
    return pl.pallas_call(
        functools.partial(kernel, R, C),
        out_shape=(
            jax.ShapeDtypeStruct((R * T, FC), bf16),
            jax.ShapeDtypeStruct((C * T, FR), bf16),
            jax.ShapeDtypeStruct((T, FC), bf16),
            jax.ShapeDtypeStruct((FC, FR), bf16),
        ),
        in_specs=[hbm, hbm, hbm],
        out_specs=(hbm, hbm, vmem, hbm),
        scratch_shapes=[
            pltpu.VMEM((FC, FR), bf16),
            pltpu.VMEM((R * T, FC), bf16),
            pltpu.VMEM((C * T, FR), bf16),
            pltpu.VMEM((C * T, FC), jnp.float32),
            pltpu.VMEM((R * T, FC), bf16),
            pltpu.VMEM(((R + 1) * T, FC), bf16),
            pltpu.VMEM((tn, R * T), bf16),
            pltpu.VMEM((2, tn, FR), bf16),
            dma((4,)), dma((2,)), dma((2,)),
            dma((2, R, PIECES)), dma((2, R, PIECES)), dma((2, R, PIECES)), dma((R, PIECES)),
            dma((2, C, PIECES)), dma((2, C, PIECES)), dma((2, C, PIECES)), dma((2, C, PIECES)), dma((PIECES,)),
            dma((R + 1, PIECES)), dma((R, PIECES)),
        ],
        compiler_params=pltpu.CompilerParams(
            collective_id=0, has_side_effects=True, vmem_limit_bytes=56 * 1024 * 1024
        ),
        cost_estimate=pl.CostEstimate(
            flops=4 * C * T * FC * FR, bytes_accessed=4 * FC * FR, transcendentals=0
        ),
    )(context, d_out, out_weight)


def add_half_kernel(context, grad, half, out):
    turned = context[...].T
    tn = 512 if grad.shape[1] % 512 == 0 else 256

    @pl.loop(0, grad.shape[1] // tn)
    def _(j):
        columns = pl.ds(pl.multiple_of(j * tn, tn), tn)
        product = jnp.dot(turned, grad[:, columns], preferred_element_type=jnp.float32)
        out[:, columns] = (half[:, columns].astype(jnp.float32) + product).astype(jnp.bfloat16)


def add_half(context, grad, half):
    K, FC = context.shape
    FR = grad.shape[1]
    tm = 256
    stripe = pl.BlockSpec((tm, FR), lambda i: (i, 0))
    return pl.pallas_call(
        add_half_kernel,
        grid=(FC // tm,),
        out_shape=jax.ShapeDtypeStruct((FC, FR), jnp.bfloat16),
        in_specs=[pl.BlockSpec((K, tm), lambda i: (0, i)), pl.BlockSpec((K, FR), lambda i: (0, 0)), stripe],
        out_specs=stripe,
        compiler_params=pltpu.CompilerParams(vmem_limit_bytes=32 * 1024 * 1024),
        cost_estimate=pl.CostEstimate(
            flops=2 * K * FC * FR, bytes_accessed=4 * FC * FR, transcendentals=0
        ),
    )(context, grad, half)


def on_device(R, C, context, d_out, out_weight):
    context_rows, grad_rows, d_context, half_weight = exchange(R, C, context, d_out, out_weight)
    d_weight = add_half(context_rows, grad_rows, half_weight)
    return (d_context, d_weight)


def solution(mesh):
    in_specs = (P(("depth", "row"), "col"), P(("depth", "col"), "row"), P("col", "row"))
    out_specs = (P(("depth", "row"), "col"), P("col", "row"))
    return jax.shard_map(
        functools.partial(on_device, mesh.shape["row"], mesh.shape["col"]),
        mesh=mesh, in_specs=in_specs, out_specs=out_specs, check_vma=False,
    )
```
